256 devices in a mesh: pat: 32 (over x, y, core), code: 8 (over z).
Axes of the slice: x: 4, y: 4, z: 8, core: 2. Of those that a mesh axis runs over, the one named last changes fastest.
Arguments:
- visit_codes: bfloat16 [2048, 128, 4096], P('pat', None, 'code'), may hold values from -6 to 6
- slice_length: int32 [512], P('pat'), may hold values from 16 to 512, as said below
- code_factor: bfloat16 [4096, 128], P('code'), may hold values from -0.09375 to 0.09375
- mix_factor: bfloat16 [128, 128], replicated, may hold values from -0.5 to 0.5
- slice_weight: float32 [512, 128], P('pat'), may hold values from 0.3 to 3
Outputs:
- mttkrp_mix: float32 [128, 128], replicated
- mttkrp_code: float32 [4096, 128], P('code')
- mttkrp_slice: float32 [512, 128], P('pat')
The draws below stay inside these ranges and needn't reach their ends.
Inputs may be any that keep to these rules, and one draw needn't show every extreme that they name: `slice_length`: every index of pat holds 16 slices whose buckets fit its 64 slots; some slice has exactly 512 visits and some exactly 16.
All inputs are finite; a program needn't handle non-finite values.
Results may differ from the reference program's by a relative error of at most 0.0011.
Values may be sent and summed in bfloat16 or wider, within the bound.
A program may use at most 128 MiB of HBM per device.

```python
import math
import jax
import jax.numpy as jnp
from jax import lax

RANK = 128
CODES = 4096
BROWS = 128
NS_STEPS = 8
SL_DEV = 16
BCAP = 64
MAXLEN = 512
LMIN = 16
SLICES = 512
BUCKETS = 2048
N_PAT = 32


def draw_slice_length(key, part):
    key = jax.random.fold_in(key, 11)
    first, second, third = jax.random.split(key, 3)
    groups = SLICES // SL_DEV
    classes = jax.random.randint(first, (groups, 1), 1, 5)
    spread = jax.random.randint(second, (groups, SL_DEV), 0, MAXLEN - LMIN + 1)
    values = (LMIN + spread * classes // 4).reshape(-1)
    picked = jax.random.randint(third, (), 0, SLICES)
    values = values.at[picked].set(MAXLEN)
    values = values.at[(picked + 1) % SLICES].set(LMIN)
    return values.astype(jnp.int32)


def block_levels(rng, shape, shards, low, high):
    def one(axis_at, parts):
        heights = jax.random.uniform(jax.random.fold_in(jax.random.fold_in(rng, 6), axis_at), (parts,), jnp.float32, low / len(shards), high / len(shards))
        return jnp.repeat(jnp.exp(heights), shape[axis_at] // parts).reshape((-1,) + (1,) * (len(shape) - axis_at - 1))

    level = one(*shards[0])
    for cut in shards[1:]:
        level = level * one(*cut)
    return level


def bell_draw(key, dims, scale, bound, cuts=(), held_as=jnp.bfloat16):
    drawn = scale * jax.random.normal(key, dims, jnp.float32)
    if cuts:
        drawn = drawn * block_levels(key, dims, cuts, -0.22, 0.18)
    return jnp.clip(drawn, -bound, bound).astype(held_as)


def setup_inputs(seed: int = 0) -> dict:
    keys = jax.random.split(jax.random.key(seed), 6)
    return {
        "visit_codes": bell_draw(keys[0], (BUCKETS, BROWS, CODES), 1.0, 6.0, ((0, 32), (2, 8))),
        "slice_length": draw_slice_length(jax.random.fold_in(keys[5], 71), 0),
        "code_factor": bell_draw(keys[2], (CODES, RANK), CODES ** -0.5, 0.09375, ((0, 8),)),
        "mix_factor": bell_draw(keys[3], (RANK, RANK), RANK ** -0.5, 0.5),
        "slice_weight": jnp.clip(jnp.exp(math.log(3.0) - 2.3025851 * jax.random.uniform(keys[4], (SLICES, RANK), jnp.float32) ** block_levels(keys[4], (SLICES, RANK), ((0, 32),), -0.2, 0.2)), 0.3, 3.0),
    }


HIGH = lax.Precision.HIGHEST

def layout(lengths):
    counts = (lengths + BROWS - 1) // BROWS
    ends = jnp.cumsum(counts)
    starts = ends - counts
    slots = jnp.arange(BCAP, dtype=jnp.int32)[:, None]
    member = (slots >= starts[None, :]) & (slots < ends[None, :])
    owner = member.astype(jnp.float32)
    first = lax.optimization_barrier(jnp.sum(jnp.where(member, starts[None, :], 0), axis=1))
    length = lax.optimization_barrier(jnp.sum(jnp.where(member, lengths[None, :], 0), axis=1))
    rowpos = (jnp.arange(BCAP, dtype=jnp.int32)[:, None] - first[:, None]) * BROWS + jnp.arange(BROWS, dtype=jnp.int32)[None, :]
    return (owner, rowpos < length[:, None])

def newton_schulz(grams):
    trace = jnp.trace(grams, axis1=1, axis2=2) + 1e-06
    ident = jnp.eye(grams.shape[1], dtype=jnp.float32)
    multi = ident[None] / jnp.sqrt(trace)[:, None, None]
    for step in range(NS_STEPS):
        inner = jnp.einsum('kar,kab,kbs->krs', multi, grams, multi, precision=HIGH)
        multi = jnp.einsum('kar,krs->kas', multi, 1.5 * ident[None] - 0.5 * inner, precision=HIGH)
    return multi

def one_group(visits, lengths, weights, code_factor, mix_factor):
    owner, live = layout(lengths)
    masked = jnp.where(live[:, :, None], visits, jnp.zeros_like(visits))
    flat = masked.reshape(-1, CODES)
    summed = jnp.dot(flat, code_factor, preferred_element_type=jnp.float32)
    mix32 = mix_factor.astype(jnp.float32)
    rowscale = jnp.dot(owner, weights, precision=HIGH)
    scaled = summed.reshape(BCAP, BROWS, RANK) * rowscale[:, None, :]
    mapped = jnp.einsum('bir,ar->bia', scaled, mix32, precision=HIGH)
    gram_b = jnp.einsum('bir,bis->brs', mapped, mapped, precision=HIGH)
    grams = jnp.einsum('bk,brs->krs', owner, gram_b, precision=HIGH)
    multi = newton_schulz(grams)
    multi_b = jnp.einsum('bk,krs->brs', owner, multi, precision=HIGH)
    polar = jnp.einsum('bir,brs->bis', mapped, multi_b, precision=HIGH).astype(jnp.bfloat16)
    cross_b = jnp.einsum('bir,bis->brs', polar.astype(jnp.float32), summed.reshape(BCAP, BROWS, RANK), precision=HIGH)
    cross = jnp.einsum('bk,brs->krs', owner, cross_b, precision=HIGH)
    mix_part = lax.optimization_barrier(jnp.sum(cross * weights[:, None, :], axis=0))
    slice_out = lax.optimization_barrier(jnp.sum(mix32[None] * cross, axis=1))
    upper = jnp.dot(polar.reshape(-1, RANK), mix_factor, preferred_element_type=jnp.float32)
    upper = (upper.reshape(BCAP, BROWS, RANK) * rowscale[:, None, :]).astype(jnp.bfloat16).reshape(-1, RANK)
    code_part = lax.dot_general(flat, upper, (((0,), (0,)), ((), ())), preferred_element_type=jnp.float32)
    return (mix_part, slice_out, code_part)

def reference(visit_codes, slice_length, code_factor, mix_factor, slice_weight):
    visits = visit_codes.reshape(N_PAT, BCAP, BROWS, CODES)
    lengths = slice_length.reshape(N_PAT, SL_DEV).astype(jnp.int32)
    weights = slice_weight.reshape(N_PAT, SL_DEV, RANK)

    def step(carry, item):
        mix_part, slice_out, code_part = one_group(item[0], item[1], item[2], code_factor, mix_factor)
        return ((carry[0] + mix_part, carry[1] + code_part), slice_out)
    init = (jnp.zeros((RANK, RANK), jnp.float32), jnp.zeros((CODES, RANK), jnp.float32))
    totals, slices = lax.scan(step, init, (visits, lengths, weights))
    return (totals[0], totals[1], slices.reshape(SLICES, RANK))
```

```python
import functools
import jax
import jax.numpy as jnp
from jax import lax
from jax.experimental import pallas as pl
from jax.experimental.pallas import tpu as pltpu
from jax.sharding import PartitionSpec as P

NS_STEPS = 8
MESH = pl.DeviceIdType.MESH
F32 = jnp.float32
BF16 = jnp.bfloat16


def dot(a, b):
    return jnp.dot(a, b, preferred_element_type=F32)


def split(a):
    high = a.astype(BF16)
    return high, (a - high.astype(F32)).astype(BF16)


def mm3(a, b):
    ah, al = split(a)
    bh, bl = split(b)
    return dot(ah, bh) + (dot(ah, bl) + dot(al, bh))


def encode(rows):
    grouped = rows.reshape(4, 32, 128)
    top = jnp.maximum(jnp.max(jnp.abs(grouped), axis=1), 1e-30)
    power = jnp.floor(jnp.log2(top) + 0.001) + 1.0
    factor = jnp.exp2(14.0 - power)
    codes = jnp.round(grouped * factor[:, None, :]).astype(jnp.int32)
    return codes.reshape(128, 128).astype(jnp.int16), power


def kernel(n_pat, n_code, x_hbm, len_ref, v_ref, h_ref, d_ref,
           mix_ref, code_ref, slice_ref,
           xv, ap, starts, rs_send, rs_recv, a_sum, u_own, u_recv, acc,
           mixp, m1, mz, m2, m3, slp, slr, acct, cbuf, hsum, rbuf,
           x_sem, rs_ss, rs_rs, ag_ss, ag_rs, m1_ss, m1_rs, m2_ss, m2_rs,
           m3_ss, m3_rs, m4_ss, m4_rs, sl_ss, sl_rs, c_ss, c_rs, r_ss, r_rs,
           g_ss, g_rs, f_ss, f_rs):
    pat = lax.axis_index("pat")
    me = lax.axis_index("code")
    chips = n_pat // 2
    chip, core = pat // 2, pat % 2
    other = pat + 1 - 2 * core

    def z_at(off):
        return lax.rem(me + off + n_code, n_code)

    def chip_at(off):
        return lax.rem(chip + off + chips, chips)

    barrier = pltpu.get_barrier_semaphore()
    for off in range(1, n_code):
        pl.semaphore_signal(barrier, inc=1, device_id=(pat, z_at(off)), device_id_type=MESH)
    pl.semaphore_signal(barrier, inc=1, device_id=(other, me), device_id_type=MESH)
    for off in range(1, chips):
        pl.semaphore_signal(barrier, inc=1, device_id=(chip_at(off) * 2 + core, me), device_id_type=MESH)

    def x_copy(i):
        part = pl.ds(i * 4, 4)
        return pltpu.make_async_copy(x_hbm.at[part], xv.at[part], x_sem.at[i])

    for i in range(16):
        x_copy(i).start()
    at = jnp.int32(0)
    for k in range(16):
        starts[k] = at
        at = at + (len_ref[k] + 127) // 128

    @pl.loop(0, 16)
    def _(i):
        x_copy(i).wait()
        part = pl.ds(i * 4, 4)
        ap[part] = dot(xv[part].reshape(512, 512), v_ref[...]).reshape(4, 128, 128)

    pl.semaphore_wait(barrier, n_code - 1 + chips)

    rowpos = lax.broadcasted_iota(jnp.int32, (128, 128), 0)

    def own(s, j):
        block = ap[jnp.minimum(starts[s] + j, 63)]
        return jnp.where(rowpos < len_ref[s] - j * 128, block, 0.0)

    def received(buf, j):
        power = buf[512:528].astype(jnp.int32).astype(F32)[4 * j:4 * j + 4]
        codes = buf[128 * j:128 * j + 128].astype(jnp.int32).astype(F32)
        return (codes.reshape(4, 32, 128) * jnp.exp2(power - 14.0)[:, None, :]).reshape(128, 128)

    def rs_copy(way, step, half):
        to = z_at(1) if way == 0 else z_at(-1)
        at = (way * 4 + step) * 2 + half
        return pltpu.make_async_remote_copy(
            src_ref=rs_send.at[at], dst_ref=rs_recv.at[at],
            send_sem=rs_ss.at[at], recv_sem=rs_rs.at[at],
            device_id=(pat, to), device_id_type=MESH)

    def rs_message(way, step, half):
        dest = z_at(4 - step) if way == 0 else z_at(step - 4)
        first = 0 if half == way else 1
        if step > first:
            rs_copy(way, step - 1, half).wait_recv()
        at = (way * 4 + step) * 2 + half
        powers = []
        for j in range(4):
            rows = own(dest * 2 + half, j)
            if step > first:
                rows = rows + received(rs_recv.at[at - 2], j)
            codes, power = encode(rows)
            rs_send[at, 128 * j:128 * j + 128] = codes
            powers.append(power)
        rs_send[at, 512:528] = jnp.concatenate(powers, axis=0).astype(jnp.int32).astype(jnp.int16)
        rs_copy(way, step, half).start()

    rs_message(0, 0, 0)
    rs_message(1, 0, 1)
    for step in range(1, 4):
        rs_message(0, step, 1)
        rs_message(1, step, 0)
        rs_message(0, step, 0)
        rs_message(1, step, 1)

    eye = (rowpos == lax.broadcasted_iota(jnp.int32, (128, 128), 1)).astype(F32)
    h32 = h_ref[...].astype(F32)
    ht = h32.T.astype(BF16)
    hd, hdt, dcol, drow = [], [], [], []
    for half in range(2):
        drow.append(d_ref[pl.ds(me * 2 + half, 1), :])
        hd.append(h32 * drow[half])
        hdt.append(hd[half].T)
        dcol.append(jnp.sum(eye * drow[half], axis=1, keepdims=True))

    grams = []
    for half in (1, 0):
        rs_copy(0, 3, half).wait_recv()
        rs_copy(1, 3, half).wait_recv()
        for j in range(4):
            rows = own(me * 2 + half, j)
            rows = rows + received(rs_recv.at[6 + half], j)
            rows = rows + received(rs_recv.at[14 + half], j)
            a_sum[half, 128 * j:128 * j + 128] = rows
    ahs, als, aths, atls = [], [], [], []
    for half in range(2):
        ah, al = split(a_sum[half])
        ath, atl = split(a_sum[half].T)
        ahs.append(ah)
        als.append(al)
        aths.append(ath)
        atls.append(atl)
        cross = dot(ath, al)
        b = dot(ath, ah) + (cross + dot(atl, ah))
        grams.append(mm3(mm3(hd[half], b), hdt[half]))

    zs, ps = [], []
    roots = []
    for half in range(2):
        trace = jnp.sum(grams[half] * eye, keepdims=True) + 1e-06
        zs.append(grams[half] / trace)
        roots.append(1.0 / jnp.sqrt(trace))
    for step in range(NS_STEPS):
        ss = [1.5 * eye - 0.5 * z for z in zs]
        if step < NS_STEPS - 1:
            zs = [mm3(z, s) for z, s in zip(zs, ss)]
        if step == 0:
            ps = [s * r for s, r in zip(ss, roots)]
        else:
            ps = [mm3(p, s) for p, s in zip(ps, ss)]
        if step < NS_STEPS - 1:
            zs = [mm3(z, s) for z, s in zip(zs, ss)]

    qts = []
    for half in range(2):
        rh, rl = split(mm3(ps[half], hd[half]))
        q = dot(rh, aths[half]) + (dot(rh, atls[half]) + dot(rl, aths[half]))
        q = q.astype(BF16)
        qts.append(q)
        u_own[half] = (dot(ht, q) * dcol[half]).astype(BF16)

    def ag_copy(way, step, half):
        to = z_at(1) if way == 0 else z_at(-1)
        at = (way * 4 + step) * 2 + half
        src = u_own.at[half] if step == 0 else u_recv.at[at - 2]
        return pltpu.make_async_remote_copy(
            src_ref=src, dst_ref=u_recv.at[at],
            send_sem=ag_ss.at[at], recv_sem=ag_rs.at[at],
            device_id=(pat, to), device_id_type=MESH)

    ag_copy(0, 0, 0).start()
    ag_copy(1, 0, 1).start()
    ag_copy(0, 0, 1).start()
    ag_copy(1, 0, 0).start()

    def code_term(u, s):
        first = starts[s]
        x = jnp.concatenate([xv[jnp.minimum(first + j, 63)] for j in range(4)], axis=0)
        return dot(u, x)

    ws = [dot(qts[half], ahs[half]) + dot(qts[half], als[half]) for half in range(2)]
    mixp[...] = ws[0] * drow[0] + ws[1] * drow[1]
    slp[...] = jnp.concatenate(
        [jnp.sum(h32 * ws[half], axis=0, keepdims=True) for half in range(2)]
        + [jnp.zeros((6, 128), F32)], axis=0)

    def sl_copy(off):
        return pltpu.make_async_remote_copy(
            src_ref=slp, dst_ref=slr.at[off - 1], send_sem=sl_ss.at[off - 1], recv_sem=sl_rs.at[off - 1],
            device_id=(pat, z_at(off)), device_id_type=MESH)

    def m1_copy(off):
        to = z_at(off)
        return pltpu.make_async_remote_copy(
            src_ref=mixp.at[pl.ds(pl.multiple_of(to * 16, 16), 16)], dst_ref=m1.at[off - 1],
            send_sem=m1_ss.at[off - 1], recv_sem=m1_rs.at[off - 1],
            device_id=(pat, to), device_id_type=MESH)

    def m2_copy():
        return pltpu.make_async_remote_copy(
            src_ref=mz, dst_ref=m2, send_sem=m2_ss, recv_sem=m2_rs,
            device_id=(other, me), device_id_type=MESH)

    def m3_copy(off, sender):
        return pltpu.make_async_remote_copy(
            src_ref=m3.at[sender], dst_ref=m3.at[sender],
            send_sem=m3_ss.at[off - 1], recv_sem=m3_rs.at[off - 1],
            device_id=(chip_at(off) * 2 + core, me), device_id_type=MESH)

    def m4_copy(off, rows):
        part = pl.ds(pl.multiple_of(rows * 16, 16), 16)
        return pltpu.make_async_remote_copy(
            src_ref=mix_ref.at[part], dst_ref=mix_ref.at[part],
            send_sem=m4_ss.at[off - 1], recv_sem=m4_rs.at[off - 1],
            device_id=(pat, z_at(off)), device_id_type=MESH)

    for off in range(1, n_code):
        m1_copy(off).start()
        sl_copy(off).start()

    acc[...] = code_term(u_own[0], me * 2) + code_term(u_own[1], me * 2 + 1)

    for step in range(4):
        for way, half in ((0, 0), (1, 1), (0, 1), (1, 0)):
            if step == 3 and half != way:
                continue
            ag_copy(way, step, half).wait_recv()
            if step < 2 or (step == 2 and half == way):
                ag_copy(way, step + 1, half).start()
            owner = z_at(-step - 1) if way == 0 else z_at(step + 1)
            acc[...] += code_term(u_recv[(way * 4 + step) * 2 + half], owner * 2 + half)
        if step == 0:
            total = mixp[pl.ds(pl.multiple_of(me * 16, 16), 16), :]
            for off in range(1, n_code):
                m1_copy(off).wait_recv()
                total = total + m1[off - 1]
            mz[...] = total
            m2_copy().start()
            slice_ref[me] = slp[0:2]
            for off in range(1, n_code):
                sl_copy(off).wait_recv()
                slice_ref[z_at(-off)] = slr[off - 1, 0:2]
        if step == 1:
            m2_copy().wait_recv()
            m3[chip] = mz[...] + m2[...]
            for off in range(1, chips):
                m3_copy(off, chip).start()
        if step == 2:
            for off in range(1, chips):
                m3_copy(off, chip_at(-off)).wait_recv()
            total = m3[0]
            for c in range(1, chips):
                total = total + m3[c]
            mix_ref[pl.ds(pl.multiple_of(me * 16, 16), 16), :] = total
            for off in range(1, n_code):
                m4_copy(off, me).start()

    acct[...] = acc[...].T.reshape(2, 256, 128)
    core_copy = pltpu.make_async_remote_copy(
        src_ref=acct.at[1 - core], dst_ref=cbuf, send_sem=c_ss, recv_sem=c_rs,
        device_id=(other, me), device_id_type=MESH)
    core_copy.start()
    core_copy.wait_recv()
    hsum[...] = (acct[core] + cbuf[...]).reshape(chips, 256 // chips, 128)

    def r_copy(off):
        to = chip_at(off)
        return pltpu.make_async_remote_copy(
            src_ref=hsum.at[to], dst_ref=rbuf.at[off - 1],
            send_sem=r_ss.at[off - 1], recv_sem=r_rs.at[off - 1],
            device_id=(to * 2 + core, me), device_id_type=MESH)

    for off in range(1, chips):
        r_copy(off).start()
    total = hsum[chip]
    for off in range(1, chips):
        r_copy(off).wait_recv()
        total = total + rbuf[off - 1]
    code_ref[core, chip] = total

    def g_copy(off, sender):
        return pltpu.make_async_remote_copy(
            src_ref=code_ref.at[core, sender], dst_ref=code_ref.at[core, sender],
            send_sem=g_ss.at[off - 1], recv_sem=g_rs.at[off - 1],
            device_id=(chip_at(off) * 2 + core, me), device_id_type=MESH)

    for off in range(1, chips):
        g_copy(off, chip).start()
    for off in range(1, chips):
        g_copy(off, chip_at(-off)).wait_recv()

    def f_copy(half):
        return pltpu.make_async_remote_copy(
            src_ref=code_ref.at[half], dst_ref=code_ref.at[half], send_sem=f_ss, recv_sem=f_rs,
            device_id=(other, me), device_id_type=MESH)

    f_copy(core).start()
    for off in range(1, n_code):
        m4_copy(off, z_at(-off)).wait_recv()

    for way in range(2):
        for step in range(4):
            for half in range(2):
                if half == way or step > 0:
                    rs_copy(way, step, half).wait_send()
                if half == way or step < 3:
                    ag_copy(way, step, half).wait_send()
    for off in range(1, n_code):
        m1_copy(off).wait_send()
        sl_copy(off).wait_send()
        m4_copy(off, me).wait_send()
    m2_copy().wait_send()
    core_copy.wait_send()
    for off in range(1, chips):
        m3_copy(off, chip).wait_send()
        r_copy(off).wait_send()
        g_copy(off, chip).wait_send()
    f_copy(core).wait_send()
    f_copy(1 - core).wait_recv()


def shards(n_pat, n_code, visit_codes, slice_length, code_factor, mix_factor, slice_weight):
    chips = n_pat // 2
    vmem = pl.BlockSpec(memory_space=pltpu.VMEM)
    dma = pltpu.SemaphoreType.DMA
    mix, code, slices = pl.pallas_call(
        functools.partial(kernel, n_pat, n_code),
        out_shape=(
            jax.ShapeDtypeStruct((128, 128), F32),
            jax.ShapeDtypeStruct((2, chips, 256 // chips, 128), F32),
            jax.ShapeDtypeStruct((n_code, 2, 128), F32),
        ),
        in_specs=[pl.BlockSpec(memory_space=pl.ANY), pl.BlockSpec(memory_space=pltpu.SMEM), vmem, vmem, vmem],
        out_specs=(vmem, vmem, vmem),
        scratch_shapes=[
            pltpu.VMEM((64, 128, 512), BF16),
            pltpu.VMEM((64, 128, 128), F32),
            pltpu.SMEM((16,), jnp.int32),
            pltpu.VMEM((16, 528, 128), jnp.int16),
            pltpu.VMEM((16, 528, 128), jnp.int16),
            pltpu.VMEM((2, 512, 128), F32),
            pltpu.VMEM((2, 128, 512), BF16),
            pltpu.VMEM((16, 128, 512), BF16),
            pltpu.VMEM((128, 512), F32),
            pltpu.VMEM((128, 128), F32),
            pltpu.VMEM((n_code - 1, 16, 128), F32),
            pltpu.VMEM((16, 128), F32),
            pltpu.VMEM((16, 128), F32),
            pltpu.VMEM((chips, 16, 128), F32),
            pltpu.VMEM((8, 128), F32),
            pltpu.VMEM((n_code - 1, 8, 128), F32),
            pltpu.VMEM((2, 256, 128), F32),
            pltpu.VMEM((256, 128), F32),
            pltpu.VMEM((chips, 256 // chips, 128), F32),
            pltpu.VMEM((chips - 1, 256 // chips, 128), F32),
            dma((16,)),
            dma((16,)), dma((16,)),
            dma((16,)), dma((16,)),
            dma((n_code - 1,)), dma((n_code - 1,)),
            dma, dma,
            dma((chips - 1,)), dma((chips - 1,)),
            dma((n_code - 1,)), dma((n_code - 1,)),
            dma((n_code - 1,)), dma((n_code - 1,)),
            dma, dma,
            dma((chips - 1,)), dma((chips - 1,)),
            dma((chips - 1,)), dma((chips - 1,)),
            dma, dma,
        ],
        compiler_params=pltpu.CompilerParams(
            collective_id=0, has_side_effects=True, vmem_limit_bytes=48 * 2**20),
        cost_estimate=pl.CostEstimate(flops=3 * 10**9, bytes_accessed=10**7, transcendentals=0),
        name="parafac2",
    )(visit_codes, slice_length, code_factor, mix_factor, slice_weight)
    return mix, code.reshape(512, 128), slices.reshape(n_code * 2, 128)


def solution(mesh):
    in_specs = (P("pat", None, "code"), P("pat"), P("code", None), P(), P("pat", None))
    out_specs = (P(), P("code", None), P("pat", None))
    body = functools.partial(shards, mesh.shape["pat"], mesh.shape["code"])
    return jax.shard_map(body, mesh=mesh, in_specs=in_specs, out_specs=out_specs, check_vma=False)
```

```python
import functools
import jax
import jax.numpy as jnp
from jax import lax
from jax.experimental import pallas as pl
from jax.experimental.pallas import tpu as pltpu
from jax.sharding import PartitionSpec as P

NS_STEPS = 8
MESH = pl.DeviceIdType.MESH
F32 = jnp.float32
BF16 = jnp.bfloat16


def dot(a, b):
    return jnp.dot(a, b, preferred_element_type=F32)


def split(a):
    high = a.astype(BF16)
    return high, (a - high.astype(F32)).astype(BF16)


def mm3(a, b):
    ah, al = split(a)
    bh, bl = split(b)
    return dot(ah, bh) + (dot(ah, bl) + dot(al, bh))


def encode(rows):
    grouped = rows.reshape(4, 32, 128)
    top = jnp.maximum(jnp.max(jnp.abs(grouped), axis=1), 1e-30)
    power = jnp.floor(jnp.log2(top) + 0.001) + 1.0
    factor = jnp.exp2(14.0 - power)
    codes = jnp.round(grouped * factor[:, None, :]).astype(jnp.int32)
    return codes.reshape(128, 128).astype(jnp.int16), power


def kernel(n_pat, n_code, x_hbm, len_hbm, v_hbm, h_hbm, d_hbm,
           mix_ref, code_ref, slice_ref,
           len_ref, v_ref, h_ref, d_ref, in_sem, xv, ap, starts, rs_send, rs_recv, a_sum, u_own, u_recv, acc,
           mixp, m2, m3s, m3r, zx, slp, acct, cbuf, hsum, rbuf,
           x_sem, rs_ss, rs_rs, ag_ss, ag_rs, zx_ss, zx_rs, m2_ss, m2_rs,
           m3_ss, m3_rs, m4_ss, m4_rs, c_ss, c_rs, r_ss, r_rs,
           g_ss, g_rs, f_ss, f_rs):
    sent = []

    def send(copy):
        copy.start()
        sent.append(copy)

    pat = lax.axis_index("pat")
    me = lax.axis_index("code")
    chips = n_pat // 2
    chip, core = pat // 2, pat % 2
    other = pat + 1 - 2 * core

    def z_at(off):
        return lax.rem(me + off + n_code, n_code)

    def chip_at(off):
        return lax.rem(chip + off + chips, chips)

    barrier = pltpu.get_barrier_semaphore()
    for off in range(1, n_code):
        pl.semaphore_signal(barrier, inc=1, device_id=(pat, z_at(off)), device_id_type=MESH)
    pl.semaphore_signal(barrier, inc=1, device_id=(other, me), device_id_type=MESH)
    for off in range(1, chips):
        pl.semaphore_signal(barrier, inc=1, device_id=(chip_at(off) * 2 + core, me), device_id_type=MESH)

    def x_copy(i):
        part = pl.ds(i * 4, 4)
        return pltpu.make_async_copy(x_hbm.at[part], xv.at[part], x_sem.at[i])

    small = [
        pltpu.make_async_copy(src, dst, in_sem.at[i])
        for i, (src, dst) in enumerate(
            [(len_hbm, len_ref), (v_hbm, v_ref), (h_hbm, h_ref), (d_hbm, d_ref)])
    ]
    small[1].start()
    x_copy(0).start()
    for i in (0, 2, 3):
        small[i].start()
    for i in range(1, 16):
        x_copy(i).start()
    for copy in small:
        copy.wait()
    at = jnp.int32(0)
    for k in range(16):
        starts[k] = at
        at = at + (len_ref[k] + 127) // 128

    @pl.loop(0, 16)
    def _(i):
        x_copy(i).wait()

    pl.semaphore_wait(barrier, n_code - 1 + chips)

    rowpos = lax.broadcasted_iota(jnp.int32, (128, 128), 0)

    def own(s, j, early=False):
        at = jnp.minimum(starts[s] + j, 63)
        block = dot(xv[at], v_ref[...]) if early else ap[at]
        return jnp.where(rowpos < len_ref[s] - j * 128, block, 0.0)

    def received(buf, j):
        power = buf[512:528].astype(jnp.int32).astype(F32)[4 * j:4 * j + 4]
        codes = buf[128 * j:128 * j + 128].astype(jnp.int32).astype(F32)
        return (codes.reshape(4, 32, 128) * jnp.exp2(power - 14.0)[:, None, :]).reshape(128, 128)

    def rs_copy(way, step, half):
        to = z_at(1) if way == 0 else z_at(-1)
        at = (way * 4 + step) * 2 + half
        return pltpu.make_async_remote_copy(
            src_ref=rs_send.at[at], dst_ref=rs_recv.at[at],
            send_sem=rs_ss.at[at], recv_sem=rs_rs.at[at],
            device_id=(pat, to), device_id_type=MESH)

    def rs_message(way, step, half):
        dest = z_at(4 - step) if way == 0 else z_at(step - 4)
        first = 0 if half == way else 1
        if step > first:
            rs_copy(way, step - 1, half).wait_recv()
        at = (way * 4 + step) * 2 + half
        powers = []
        for j in range(4):
            rows = own(dest * 2 + half, j, step <= first)
            if step > first:
                rows = rows + received(rs_recv.at[at - 2], j)
            codes, power = encode(rows)
            rs_send[at, 128 * j:128 * j + 128] = codes
            powers.append(power)
        rs_send[at, 512:528] = jnp.concatenate(powers, axis=0).astype(jnp.int32).astype(jnp.int16)
        send(rs_copy(way, step, half))

    rs_message(0, 0, 0)
    rs_message(1, 0, 1)
    rs_message(0, 1, 1)
    rs_message(1, 1, 0)

    @pl.loop(0, 16)
    def _(i):
        part = pl.ds(i * 4, 4)
        ap[part] = dot(xv[part].reshape(512, 512), v_ref[...]).reshape(4, 128, 128)

    for step in range(1, 4):
        if step > 1:
            rs_message(0, step, 1)
            rs_message(1, step, 0)
        rs_message(0, step, 0)
        rs_message(1, step, 1)

    eye = (rowpos == lax.broadcasted_iota(jnp.int32, (128, 128), 1)).astype(F32)
    h32 = h_ref[...].astype(F32)
    ht = h32.T.astype(BF16)
    hd, hdt, dcol, drow = [], [], [], []
    for half in range(2):
        drow.append(d_ref[pl.ds(me * 2 + half, 1), :])
        hd.append(h32 * drow[half])
        hdt.append(hd[half].T)
        dcol.append(jnp.sum(eye * drow[half], axis=1, keepdims=True))

    grams = []
    for half in (1, 0):
        rs_copy(0, 3, half).wait_recv()
        rs_copy(1, 3, half).wait_recv()
        for j in range(4):
            rows = own(me * 2 + half, j)
            rows = rows + received(rs_recv.at[6 + half], j)
            rows = rows + received(rs_recv.at[14 + half], j)
            a_sum[half, 128 * j:128 * j + 128] = rows
    ahs, als, aths, atls = [], [], [], []
    for half in range(2):
        ah, al = split(a_sum[half])
        ath, atl = split(a_sum[half].T)
        ahs.append(ah)
        als.append(al)
        aths.append(ath)
        atls.append(atl)
        cross = dot(ath, al)
        b = dot(ath, ah) + (cross + dot(atl, ah))
        grams.append(mm3(mm3(hd[half], b), hdt[half]))

    zs, ps = [], []
    roots = []
    for half in range(2):
        trace = jnp.sum(grams[half] * eye, keepdims=True) + 1e-06
        zs.append(grams[half] / trace)
        roots.append(1.0 / jnp.sqrt(trace))
    for step in range(NS_STEPS):
        ss = [1.5 * eye - 0.5 * z for z in zs]
        if step < NS_STEPS - 1:
            zs = [mm3(z, s) for z, s in zip(zs, ss)]
        if step == 0:
            ps = [s * r for s, r in zip(ss, roots)]
        else:
            ps = [mm3(p, s) for p, s in zip(ps, ss)]
        if step < NS_STEPS - 1:
            zs = [mm3(z, s) for z, s in zip(zs, ss)]

    qts = []
    for half in range(2):
        rh, rl = split(mm3(ps[half], hd[half]))
        q = dot(rh, aths[half]) + (dot(rh, atls[half]) + dot(rl, aths[half]))
        q = q.astype(BF16)
        qts.append(q)
        u_own[half] = (dot(ht, q) * dcol[half]).astype(BF16)

    def ag_copy(way, step, half):
        to = z_at(1) if way == 0 else z_at(-1)
        at = (way * 4 + step) * 2 + half
        src = u_own.at[half] if step == 0 else u_recv.at[at - 2]
        return pltpu.make_async_remote_copy(
            src_ref=src, dst_ref=u_recv.at[at],
            send_sem=ag_ss.at[at], recv_sem=ag_rs.at[at],
            device_id=(pat, to), device_id_type=MESH)

    send(ag_copy(0, 0, 0))
    send(ag_copy(1, 0, 1))
    send(ag_copy(0, 0, 1))
    send(ag_copy(1, 0, 0))

    def code_term(u, s):
        first = starts[s]
        x = jnp.concatenate([xv[jnp.minimum(first + j, 63)] for j in range(4)], axis=0)
        return dot(u, x)

    ws = [dot(qts[half], ahs[half]) + dot(qts[half], als[half]) for half in range(2)]
    mixp[...] = ws[0] * drow[0] + ws[1] * drow[1]
    slp[...] = jnp.concatenate(
        [jnp.sum(h32 * ws[half], axis=0, keepdims=True) for half in range(2)]
        + [jnp.zeros((6, 128), F32)], axis=0)

    def m2_copy():
        return pltpu.make_async_remote_copy(
            src_ref=mixp, dst_ref=m2, send_sem=m2_ss, recv_sem=m2_rs,
            device_id=(other, me), device_id_type=MESH)

    def m3_copy(off):
        to = chip_at(off)
        return pltpu.make_async_remote_copy(
            src_ref=m3s.at[to], dst_ref=m3r.at[chip],
            send_sem=m3_ss.at[off - 1], recv_sem=m3_rs.at[off - 1],
            device_id=(to * 2 + core, me), device_id_type=MESH)

    def zx_copy(off):
        return pltpu.make_async_remote_copy(
            src_ref=zx.at[me], dst_ref=zx.at[me],
            send_sem=zx_ss.at[off - 1], recv_sem=zx_rs.at[off - 1],
            device_id=(pat, z_at(off)), device_id_type=MESH)

    mix_rows = 128 // chips

    def m4_copy(off):
        at = pl.ds(pl.multiple_of(chip * mix_rows, mix_rows), mix_rows)
        return pltpu.make_async_remote_copy(
            src_ref=mix_ref.at[at], dst_ref=mix_ref.at[at],
            send_sem=m4_ss.at[off - 1], recv_sem=m4_rs.at[off - 1],
            device_id=(chip_at(off) * 2 + core, me), device_id_type=MESH)

    send(m2_copy())
    acc[...] = code_term(u_own[0], me * 2) + code_term(u_own[1], me * 2 + 1)

    for step in range(4):
        for way, half in ((0, 0), (1, 1), (0, 1), (1, 0)):
            if step == 3 and half != way:
                continue
            ag_copy(way, step, half).wait_recv()
            if step < 2 or (step == 2 and half == way):
                send(ag_copy(way, step + 1, half))
            owner = z_at(-step - 1) if way == 0 else z_at(step + 1)
            acc[...] += code_term(u_recv[(way * 4 + step) * 2 + half], owner * 2 + half)
            if (step, way, half) == (0, 1, 1):
                m2_copy().wait_recv()
                m3s[...] = (mixp[...] + m2[...]).reshape(chips, mix_rows, 128)
                m3r[chip] = m3s[chip]
                for off in range(1, chips):
                    send(m3_copy(off))
            if (step, way, half) == (2, 1, 1):
                for off in range(1, chips):
                    m3_copy(off).wait_recv()
                total = m3r[0]
                for c in range(1, chips):
                    total = total + m3r[c]
                zx[me, 0:mix_rows] = total
                zx[me, mix_rows:mix_rows + 8] = slp[...]

    acct[...] = acc[...].T.reshape(2, 256, 128)
    core_copy = pltpu.make_async_remote_copy(
        src_ref=acct.at[1 - core], dst_ref=cbuf, send_sem=c_ss, recv_sem=c_rs,
        device_id=(other, me), device_id_type=MESH)
    send(core_copy)
    for off in range(1, n_code):
        send(zx_copy(off))
    core_copy.wait_recv()
    hsum[...] = (acct[core] + cbuf[...]).reshape(chips, 256 // chips, 128)

    def r_copy(off):
        to = chip_at(off)
        return pltpu.make_async_remote_copy(
            src_ref=hsum.at[to], dst_ref=rbuf.at[off - 1],
            send_sem=r_ss.at[off - 1], recv_sem=r_rs.at[off - 1],
            device_id=(to * 2 + core, me), device_id_type=MESH)

    for off in range(1, chips):
        send(r_copy(off))
    for off in range(1, n_code):
        zx_copy(off).wait_recv()
    total = zx[0, 0:mix_rows]
    for z in range(1, n_code):
        total = total + zx[z, 0:mix_rows]
    mix_ref[pl.ds(pl.multiple_of(chip * mix_rows, mix_rows), mix_rows), :] = total
    for off in range(1, chips):
        send(m4_copy(off))
    for z in range(n_code):
        slice_ref[z] = zx[z, mix_rows:mix_rows + 2]
    total = hsum[chip]
    for off in range(1, chips):
        r_copy(off).wait_recv()
        total = total + rbuf[off - 1]
    code_ref[core, chip] = total

    def g_copy(off, sender):
        return pltpu.make_async_remote_copy(
            src_ref=code_ref.at[core, sender], dst_ref=code_ref.at[core, sender],
            send_sem=g_ss.at[off - 1], recv_sem=g_rs.at[off - 1],
            device_id=(chip_at(off) * 2 + core, me), device_id_type=MESH)

    for off in range(1, chips):
        send(g_copy(off, chip))
    for off in range(1, chips):
        g_copy(off, chip_at(-off)).wait_recv()

    def f_copy(half):
        return pltpu.make_async_remote_copy(
            src_ref=code_ref.at[half], dst_ref=code_ref.at[half], send_sem=f_ss, recv_sem=f_rs,
            device_id=(other, me), device_id_type=MESH)

    send(f_copy(core))
    for off in range(1, chips):
        m4_copy(off).wait_recv()

    for copy in sent:
        copy.wait_send()
    f_copy(1 - core).wait_recv()


def shards(n_pat, n_code, visit_codes, slice_length, code_factor, mix_factor, slice_weight):
    chips = n_pat // 2
    vmem = pl.BlockSpec(memory_space=pltpu.VMEM)
    dma = pltpu.SemaphoreType.DMA
    mix, code, slices = pl.pallas_call(
        functools.partial(kernel, n_pat, n_code),
        out_shape=(
            jax.ShapeDtypeStruct((128, 128), F32),
            jax.ShapeDtypeStruct((2, chips, 256 // chips, 128), F32),
            jax.ShapeDtypeStruct((n_code, 2, 128), F32),
        ),
        in_specs=[pl.BlockSpec(memory_space=pltpu.HBM)] * 5,
        out_specs=(vmem, vmem, vmem),
        scratch_shapes=[
            pltpu.SMEM((16,), jnp.int32),
            pltpu.VMEM((512, 128), BF16),
            pltpu.VMEM((128, 128), BF16),
            pltpu.VMEM((16, 128), F32),
            dma((4,)),
            pltpu.VMEM((64, 128, 512), BF16),
            pltpu.VMEM((64, 128, 128), F32),
            pltpu.SMEM((16,), jnp.int32),
            pltpu.VMEM((16, 528, 128), jnp.int16),
            pltpu.VMEM((16, 528, 128), jnp.int16),
            pltpu.VMEM((2, 512, 128), F32),
            pltpu.VMEM((2, 128, 512), BF16),
            pltpu.VMEM((16, 128, 512), BF16),
            pltpu.VMEM((128, 512), F32),
            pltpu.VMEM((128, 128), F32),
            pltpu.VMEM((128, 128), F32),
            pltpu.VMEM((chips, 128 // chips, 128), F32),
            pltpu.VMEM((chips, 128 // chips, 128), F32),
            pltpu.VMEM((n_code, 128 // chips + 8, 128), F32),
            pltpu.VMEM((8, 128), F32),
            pltpu.VMEM((2, 256, 128), F32),
            pltpu.VMEM((256, 128), F32),
            pltpu.VMEM((chips, 256 // chips, 128), F32),
            pltpu.VMEM((chips - 1, 256 // chips, 128), F32),
            dma((16,)),
            dma((16,)), dma((16,)),
            dma((16,)), dma((16,)),
            dma((n_code - 1,)), dma((n_code - 1,)),
            dma, dma,
            dma((chips - 1,)), dma((chips - 1,)),
            dma((chips - 1,)), dma((chips - 1,)),
            dma, dma,
            dma((chips - 1,)), dma((chips - 1,)),
            dma((chips - 1,)), dma((chips - 1,)),
            dma, dma,
        ],
        compiler_params=pltpu.CompilerParams(
            collective_id=0, has_side_effects=True, vmem_limit_bytes=48 * 2**20),
        cost_estimate=pl.CostEstimate(flops=3 * 10**9, bytes_accessed=10**7, transcendentals=0),
        name="parafac2",
    )(visit_codes, slice_length, code_factor, mix_factor, slice_weight)
    return mix, code.reshape(512, 128), slices.reshape(n_code * 2, 128)


def solution(mesh):
    in_specs = (P("pat", None, "code"), P("pat"), P("code", None), P(), P("pat", None))
    out_specs = (P(), P("code", None), P("pat", None))
    body = functools.partial(shards, mesh.shape["pat"], mesh.shape["code"])
    return jax.shard_map(body, mesh=mesh, in_specs=in_specs, out_specs=out_specs, check_vma=False)
```

```python
import functools
import jax
import jax.numpy as jnp
from jax import lax
from jax.experimental import pallas as pl
from jax.experimental.pallas import tpu as pltpu
from jax.sharding import PartitionSpec as P

NS_STEPS = 8
MESH = pl.DeviceIdType.MESH
F32 = jnp.float32
BF16 = jnp.bfloat16


def dot(a, b):
    return jnp.dot(a, b, preferred_element_type=F32)


def split(a):
    high = a.astype(BF16)
    return high, (a - high.astype(F32)).astype(BF16)


def mm3(a, b):
    ah, al = split(a)
    bh, bl = split(b)
    return dot(ah, bh) + (dot(ah, bl) + dot(al, bh))


def encode(rows):
    grouped = rows.reshape(4, 32, 128)
    top = jnp.maximum(jnp.max(jnp.abs(grouped), axis=1), 1e-30)
    power = jnp.floor(jnp.log2(top) + 0.001) + 1.0
    factor = jnp.exp2(14.0 - power)
    codes = jnp.round(grouped * factor[:, None, :]).astype(jnp.int32)
    return codes.reshape(128, 128).astype(jnp.int16), power


def kernel(n_pat, n_code, x_hbm, len_hbm, v_hbm, h_hbm, d_hbm,
           mix_ref, code_ref, slice_ref,
           len_ref, v_ref, h_ref, d_ref, in_sem, xv, ap, starts, rs_send, rs_recv, a_sum, u_own, u_recv, acc,
           mixp, m2, m3s, m3r, zx, slp, acct, cbuf, hsum, rbuf,
           x_sem, rs_ss, rs_rs, ag_ss, ag_rs, zx_ss, zx_rs, m2_ss, m2_rs,
           m3_ss, m3_rs, m4_ss, m4_rs, c_ss, c_rs, r_ss, r_rs,
           g_ss, g_rs, f_ss, f_rs):
    sent = []

    def send(copy):
        copy.start()
        sent.append(copy)

    pat = lax.axis_index("pat")
    me = lax.axis_index("code")
    chips = n_pat // 2
    chip, core = pat // 2, pat % 2
    other = pat + 1 - 2 * core

    def z_at(off):
        return lax.rem(me + off + n_code, n_code)

    def chip_at(off):
        return lax.rem(chip + off + chips, chips)

    def x_copy(i):
        part = pl.ds(i * 4, 4)
        return pltpu.make_async_copy(x_hbm.at[part], xv.at[part], x_sem.at[i])

    small = [
        pltpu.make_async_copy(src, dst, in_sem.at[i])
        for i, (src, dst) in enumerate(
            [(len_hbm, len_ref), (v_hbm, v_ref), (h_hbm, h_ref), (d_hbm, d_ref)])
    ]
    small[1].start()
    x_copy(0).start()
    for i in (0, 2, 3):
        small[i].start()
    for i in range(1, 16):
        x_copy(i).start()
    barrier = pltpu.get_barrier_semaphore()
    for off in range(1, n_code):
        pl.semaphore_signal(barrier, inc=1, device_id=(pat, z_at(off)), device_id_type=MESH)
    pl.semaphore_signal(barrier, inc=1, device_id=(other, me), device_id_type=MESH)
    for off in range(1, chips):
        pl.semaphore_signal(barrier, inc=1, device_id=(chip_at(off) * 2 + core, me), device_id_type=MESH)

    for copy in small:
        copy.wait()
    at = jnp.int32(0)
    for k in range(16):
        starts[k] = at
        at = at + (len_ref[k] + 127) // 128

    @pl.loop(0, 16)
    def _(i):
        x_copy(i).wait()

    pl.semaphore_wait(barrier, n_code - 1 + chips)

    rowpos = lax.broadcasted_iota(jnp.int32, (128, 128), 0)

    def own(s, j, early=False):
        at = jnp.minimum(starts[s] + j, 63)
        block = dot(xv[at], v_ref[...]) if early else ap[at]
        return jnp.where(rowpos < len_ref[s] - j * 128, block, 0.0)

    def received(buf, j):
        power = buf[512:528].astype(jnp.int32).astype(F32)[4 * j:4 * j + 4]
        codes = buf[128 * j:128 * j + 128].astype(jnp.int32).astype(F32)
        return (codes.reshape(4, 32, 128) * jnp.exp2(power - 14.0)[:, None, :]).reshape(128, 128)

    def rs_copy(way, step, half):
        to = z_at(1) if way == 0 else z_at(-1)
        at = (way * 4 + step) * 2 + half
        return pltpu.make_async_remote_copy(
            src_ref=rs_send.at[at], dst_ref=rs_recv.at[at],
            send_sem=rs_ss.at[at], recv_sem=rs_rs.at[at],
            device_id=(pat, to), device_id_type=MESH)

    def rs_message(way, step, half):
        dest = z_at(4 - step) if way == 0 else z_at(step - 4)
        first = 0 if half == way else 1
        if step > first:
            rs_copy(way, step - 1, half).wait_recv()
        at = (way * 4 + step) * 2 + half
        powers = []
        for j in range(4):
            rows = own(dest * 2 + half, j, step <= first)
            if step > first:
                rows = rows + received(rs_recv.at[at - 2], j)
            codes, power = encode(rows)
            rs_send[at, 128 * j:128 * j + 128] = codes
            powers.append(power)
        rs_send[at, 512:528] = jnp.concatenate(powers, axis=0).astype(jnp.int32).astype(jnp.int16)
        send(rs_copy(way, step, half))

    rs_message(0, 0, 0)
    rs_message(1, 0, 1)
    rs_message(0, 1, 1)
    rs_message(1, 1, 0)

    @pl.loop(0, 16)
    def _(i):
        part = pl.ds(i * 4, 4)
        ap[part] = dot(xv[part].reshape(512, 512), v_ref[...]).reshape(4, 128, 128)

    for step in range(1, 4):
        if step > 1:
            rs_message(0, step, 1)
            rs_message(1, step, 0)
        rs_message(0, step, 0)
        rs_message(1, step, 1)

    eye = (rowpos == lax.broadcasted_iota(jnp.int32, (128, 128), 1)).astype(F32)
    h32 = h_ref[...].astype(F32)
    ht = h32.T.astype(BF16)
    hd, hdt, dcol, drow = [], [], [], []
    for half in range(2):
        drow.append(d_ref[pl.ds(me * 2 + half, 1), :])
        hd.append(h32 * drow[half])
        hdt.append(hd[half].T)
        dcol.append(jnp.sum(eye * drow[half], axis=1, keepdims=True))

    grams = []
    for half in range(2):
        rs_copy(1 - half, 3, half).wait_recv()
        for j in range(4):
            rows = own(me * 2 + half, j) + received(rs_recv.at[(1 - half) * 8 + 6 + half], j)
            a_sum[half, 128 * j:128 * j + 128] = rows
    for half in range(2):
        rs_copy(half, 3, half).wait_recv()
        for j in range(4):
            a_sum[half, 128 * j:128 * j + 128] += received(rs_recv.at[half * 8 + 6 + half], j)
    ahs, als, aths, atls = [], [], [], []
    for half in range(2):
        ah, al = split(a_sum[half])
        ath, atl = split(a_sum[half].T)
        ahs.append(ah)
        als.append(al)
        aths.append(ath)
        atls.append(atl)
        cross = dot(ath, al)
        b = dot(ath, ah) + (cross + dot(atl, ah))
        grams.append(mm3(mm3(hd[half], b), hdt[half]))

    zs, ps = [], []
    roots = []
    for half in range(2):
        trace = jnp.sum(grams[half] * eye, keepdims=True) + 1e-06
        zs.append(grams[half] / trace)
        roots.append(1.0 / jnp.sqrt(trace))
    for step in range(NS_STEPS):
        ss = [1.5 * eye - 0.5 * z for z in zs]
        if step < NS_STEPS - 1:
            zs = [mm3(z, s) for z, s in zip(zs, ss)]
        if step == 0:
            ps = [s * r for s, r in zip(ss, roots)]
        else:
            ps = [mm3(p, s) for p, s in zip(ps, ss)]
        if step < NS_STEPS - 1:
            zs = [mm3(z, s) for z, s in zip(zs, ss)]

    qts = []
    for half in range(2):
        rh, rl = split(mm3(ps[half], hd[half]))
        q = dot(rh, aths[half]) + (dot(rh, atls[half]) + dot(rl, aths[half]))
        q = q.astype(BF16)
        qts.append(q)
        u_own[half] = (dot(ht, q) * dcol[half]).astype(BF16)

    def ag_copy(way, step, half):
        to = z_at(1) if way == 0 else z_at(-1)
        at = (way * 4 + step) * 2 + half
        src = u_own.at[half] if step == 0 else u_recv.at[at - 2]
        return pltpu.make_async_remote_copy(
            src_ref=src, dst_ref=u_recv.at[at],
            send_sem=ag_ss.at[at], recv_sem=ag_rs.at[at],
            device_id=(pat, to), device_id_type=MESH)

    send(ag_copy(0, 0, 0))
    send(ag_copy(1, 0, 1))
    send(ag_copy(0, 0, 1))
    send(ag_copy(1, 0, 0))

    def code_term(u, s):
        first = starts[s]
        x = jnp.concatenate([xv[jnp.minimum(first + j, 63)] for j in range(4)], axis=0)
        return dot(u, x)

    ws = [dot(qts[half], ahs[half]) + dot(qts[half], als[half]) for half in range(2)]
    mixp[...] = ws[0] * drow[0] + ws[1] * drow[1]
    slp[...] = jnp.concatenate(
        [jnp.sum(h32 * ws[half], axis=0, keepdims=True) for half in range(2)]
        + [jnp.zeros((6, 128), F32)], axis=0)

    def m2_copy():
        return pltpu.make_async_remote_copy(
            src_ref=mixp, dst_ref=m2, send_sem=m2_ss, recv_sem=m2_rs,
            device_id=(other, me), device_id_type=MESH)

    def m3_copy(off):
        to = chip_at(off)
        return pltpu.make_async_remote_copy(
            src_ref=m3s.at[to], dst_ref=m3r.at[chip],
            send_sem=m3_ss.at[off - 1], recv_sem=m3_rs.at[off - 1],
            device_id=(to * 2 + core, me), device_id_type=MESH)

    def zx_copy(off):
        return pltpu.make_async_remote_copy(
            src_ref=zx.at[me], dst_ref=zx.at[me],
            send_sem=zx_ss.at[off - 1], recv_sem=zx_rs.at[off - 1],
            device_id=(pat, z_at(off)), device_id_type=MESH)

    mix_rows = 128 // chips

    def m4_copy(off):
        at = pl.ds(pl.multiple_of(chip * mix_rows, mix_rows), mix_rows)
        return pltpu.make_async_remote_copy(
            src_ref=mix_ref.at[at], dst_ref=mix_ref.at[at],
            send_sem=m4_ss.at[off - 1], recv_sem=m4_rs.at[off - 1],
            device_id=(chip_at(off) * 2 + core, me), device_id_type=MESH)

    send(m2_copy())
    acc[...] = code_term(u_own[0], me * 2) + code_term(u_own[1], me * 2 + 1)

    for step in range(4):
        for way, half in ((0, 0), (1, 1), (0, 1), (1, 0)):
            if step == 3 and half != way:
                continue
            ag_copy(way, step, half).wait_recv()
            if step < 2 or (step == 2 and half == way):
                send(ag_copy(way, step + 1, half))
            owner = z_at(-step - 1) if way == 0 else z_at(step + 1)
            acc[...] += code_term(u_recv[(way * 4 + step) * 2 + half], owner * 2 + half)
            if (step, way, half) == (0, 1, 1):
                m2_copy().wait_recv()
                m3s[...] = (mixp[...] + m2[...]).reshape(chips, mix_rows, 128)
                m3r[chip] = m3s[chip]
                for off in range(1, chips):
                    send(m3_copy(off))
            if (step, way, half) == (2, 1, 1):
                for off in range(1, chips):
                    m3_copy(off).wait_recv()
                total = m3r[0]
                for c in range(1, chips):
                    total = total + m3r[c]
                zx[me, 0:mix_rows] = total
                zx[me, mix_rows:mix_rows + 8] = slp[...]

    acct[...] = acc[...].T.reshape(2, 256, 128)
    core_copy = pltpu.make_async_remote_copy(
        src_ref=acct.at[1 - core], dst_ref=cbuf, send_sem=c_ss, recv_sem=c_rs,
        device_id=(other, me), device_id_type=MESH)
    send(core_copy)
    for off in range(1, n_code):
        send(zx_copy(off))
    core_copy.wait_recv()
    hsum[...] = (acct[core] + cbuf[...]).reshape(chips, 256 // chips, 128)

    def r_copy(off):
        to = chip_at(off)
        return pltpu.make_async_remote_copy(
            src_ref=hsum.at[to], dst_ref=rbuf.at[off - 1],
            send_sem=r_ss.at[off - 1], recv_sem=r_rs.at[off - 1],
            device_id=(to * 2 + core, me), device_id_type=MESH)

    for off in range(1, chips):
        send(r_copy(off))
    for off in range(1, n_code):
        zx_copy(off).wait_recv()
    total = zx[0, 0:mix_rows]
    for z in range(1, n_code):
        total = total + zx[z, 0:mix_rows]
    mix_ref[pl.ds(pl.multiple_of(chip * mix_rows, mix_rows), mix_rows), :] = total
    for off in range(1, chips):
        send(m4_copy(off))
    for z in range(n_code):
        slice_ref[z] = zx[z, mix_rows:mix_rows + 2]
    total = hsum[chip]
    for off in range(1, chips):
        r_copy(off).wait_recv()
        total = total + rbuf[off - 1]
    code_ref[core, chip] = total

    def g_copy(off, sender):
        return pltpu.make_async_remote_copy(
            src_ref=code_ref.at[core, sender], dst_ref=code_ref.at[core, sender],
            send_sem=g_ss.at[off - 1], recv_sem=g_rs.at[off - 1],
            device_id=(chip_at(off) * 2 + core, me), device_id_type=MESH)

    for off in range(1, chips):
        send(g_copy(off, chip))
    for off in range(1, chips):
        g_copy(off, chip_at(-off)).wait_recv()

    def f_copy(half):
        return pltpu.make_async_remote_copy(
            src_ref=code_ref.at[half], dst_ref=code_ref.at[half], send_sem=f_ss, recv_sem=f_rs,
            device_id=(other, me), device_id_type=MESH)

    send(f_copy(core))
    for off in range(1, chips):
        m4_copy(off).wait_recv()

    for copy in sent:
        copy.wait_send()
    f_copy(1 - core).wait_recv()


def shards(n_pat, n_code, visit_codes, slice_length, code_factor, mix_factor, slice_weight):
    chips = n_pat // 2
    vmem = pl.BlockSpec(memory_space=pltpu.VMEM)
    dma = pltpu.SemaphoreType.DMA
    mix, code, slices = pl.pallas_call(
        functools.partial(kernel, n_pat, n_code),
        out_shape=(
            jax.ShapeDtypeStruct((128, 128), F32),
            jax.ShapeDtypeStruct((2, chips, 256 // chips, 128), F32),
            jax.ShapeDtypeStruct((n_code, 2, 128), F32),
        ),
        in_specs=[pl.BlockSpec(memory_space=pltpu.HBM)] * 5,
        out_specs=(vmem, vmem, vmem),
        scratch_shapes=[
            pltpu.SMEM((16,), jnp.int32),
            pltpu.VMEM((512, 128), BF16),
            pltpu.VMEM((128, 128), BF16),
            pltpu.VMEM((16, 128), F32),
            dma((4,)),
            pltpu.VMEM((64, 128, 512), BF16),
            pltpu.VMEM((64, 128, 128), F32),
            pltpu.SMEM((16,), jnp.int32),
            pltpu.VMEM((16, 528, 128), jnp.int16),
            pltpu.VMEM((16, 528, 128), jnp.int16),
            pltpu.VMEM((2, 512, 128), F32),
            pltpu.VMEM((2, 128, 512), BF16),
            pltpu.VMEM((16, 128, 512), BF16),
            pltpu.VMEM((128, 512), F32),
            pltpu.VMEM((128, 128), F32),
            pltpu.VMEM((128, 128), F32),
            pltpu.VMEM((chips, 128 // chips, 128), F32),
            pltpu.VMEM((chips, 128 // chips, 128), F32),
            pltpu.VMEM((n_code, 128 // chips + 8, 128), F32),
            pltpu.VMEM((8, 128), F32),
            pltpu.VMEM((2, 256, 128), F32),
            pltpu.VMEM((256, 128), F32),
            pltpu.VMEM((chips, 256 // chips, 128), F32),
            pltpu.VMEM((chips - 1, 256 // chips, 128), F32),
            dma((16,)),
            dma((16,)), dma((16,)),
            dma((16,)), dma((16,)),
            dma((n_code - 1,)), dma((n_code - 1,)),
            dma, dma,
            dma((chips - 1,)), dma((chips - 1,)),
            dma((chips - 1,)), dma((chips - 1,)),
            dma, dma,
            dma((chips - 1,)), dma((chips - 1,)),
            dma((chips - 1,)), dma((chips - 1,)),
            dma, dma,
        ],
        compiler_params=pltpu.CompilerParams(
            collective_id=0, has_side_effects=True, vmem_limit_bytes=48 * 2**20),
        cost_estimate=pl.CostEstimate(flops=3 * 10**9, bytes_accessed=10**7, transcendentals=0),
        name="parafac2",
    )(visit_codes, slice_length, code_factor, mix_factor, slice_weight)
    return mix, code.reshape(512, 128), slices.reshape(n_code * 2, 128)


def solution(mesh):
    in_specs = (P("pat", None, "code"), P("pat"), P("code", None), P(), P("pat", None))
    out_specs = (P(), P("code", None), P("pat", None))
    body = functools.partial(shards, mesh.shape["pat"], mesh.shape["code"])
    return jax.shard_map(body, mesh=mesh, in_specs=in_specs, out_specs=out_specs, check_vma=False)
```
